32 devices in a mesh: shot: 2 (over x), gx: 4 (over y, core), gy: 4 (over z).
Axes of the slice: x: 2, y: 2, z: 4, core: 2. Of those that a mesh axis runs over, the one named last changes fastest.
Arguments:
- forward: bfloat16 [2, 2, 9, 16, 512, 512], P('shot', None, None, None, 'gx', 'gy'), may hold values from -6 to 6
- adjoint: bfloat16 [2, 2, 9, 16, 512, 512], P('shot', None, None, None, 'gx', 'gy'), may hold values from -6 to 6
- snap_times: int32 [2, 2], P('shot'), may hold values from 1 to 32, as said below
- sources: int32 [2, 2], P('shot'), may hold values from 0 to 511
- aperture: int32 [2, 4, 4], P('shot', 'gx', 'gy'), may hold values 0 or 1
Outputs:
- smoothed: float32 [3, 16, 512, 512], P(None, 'shot', 'gx', 'gy')
The draws below stay inside these ranges and needn't reach their ends.
Inputs may be any that keep to these rules, and one draw needn't show every extreme that they name: `snap_times`: each shot's times rise strictly, the first and every step from one to the next being 1 to 16; some shot takes steps of 16 throughout.
All inputs are finite; a program needn't handle non-finite values. No bound on the sum of `aperture` on one device may be relied on, other than what follows from the above.
Results may differ from the reference program's by a relative error of at most 0.0003.
Values sent between devices are 32-bit elements; how exact they have to be, the bound alone decides.
A program may use at most 64 MiB of HBM per device.

```python
import jax
import jax.numpy as jnp
from jax import lax

CX = 128
CY = 128
LEV = 16
SNAPS = 2
COMPS = 9
RADIUS = 16
SHOTS = 2
NX = 512
NY = 512
MUTE = 32
N_GX = 4
N_GY = 4


def draw_snap_times(key, part):
    step_sizes = jax.random.randint(jax.random.fold_in(key, 11), (SHOTS, SNAPS), 1, 17)
    full_shot = jax.random.randint(jax.random.fold_in(key, 12), (), 0, SHOTS)
    short_shot = (full_shot + 1) % SHOTS
    shot_ids = jnp.arange(SHOTS)[:, None]
    snap_ids = jnp.arange(SNAPS)[None, :]
    step_sizes = jnp.where(shot_ids == full_shot, 16, step_sizes)
    step_sizes = jnp.where((shot_ids == short_shot) & (snap_ids == 0), 1, step_sizes)
    return jnp.cumsum(step_sizes, axis=1).astype(jnp.int32)


def plant(drawn, own_key, low, top_value):
    shape = drawn.shape
    index_at = [jax.random.randint(jax.random.fold_in(own_key, axis), (), 0, shape[axis]) for axis in range(len(shape))]
    drawn = drawn.at[tuple(index_at)].set(low)
    longest = shape.index(max(shape))
    index_at[longest] = (index_at[longest] + 1) % shape[longest]
    return drawn.at[tuple(index_at)].set(top_value)


def strengthened(array, key, source, target, parts, factor):
    owner, partner = [(jnp.arange(array.shape[dim]) // (array.shape[dim] // parts)).reshape([-1 if axis == dim else 1 for axis in range(array.ndim)]) for dim in (source, target)]
    chosen = jax.random.permutation(key, parts)[partner]
    strong = (owner == chosen) | (owner == (partner + parts // 2) % parts)
    return jnp.where(strong, factor * array, array)


def block_scale(own_key, extent, cuts, smallest, largest):
    def one(axis_at, blocks):
        steps = jax.random.uniform(jax.random.fold_in(jax.random.fold_in(own_key, 6), axis_at), (blocks,), jnp.float32, smallest / len(cuts), largest / len(cuts))
        return jnp.repeat(jnp.exp(steps), extent[axis_at] // blocks).reshape((-1,) + (1,) * (len(extent) - axis_at - 1))

    level = one(*cuts[0])
    for cut in cuts[1:]:
        level = level * one(*cut)
    return level


def scatter_about(rng, shape, scale, most, shards=(), kind=jnp.bfloat16):
    drawn = jax.random.normal(rng, shape, jnp.float32) * scale
    if len(shards) > 0:
        drawn = block_scale(rng, shape, shards, -0.22, 0.18) * drawn
    return jnp.clip(drawn, min=-most, max=most).astype(kind)


def heavy_noise(stream_key, extent, scale, most, pieces, heavy, held_as=jnp.bfloat16):
    entries = scale * jax.random.normal(stream_key, extent, jnp.float32)
    if pieces:
        entries = entries * block_scale(stream_key, extent, pieces, -0.22, 0.18)
    return jnp.clip(strengthened(entries, jax.random.fold_in(stream_key, 3), *heavy), -most, most).astype(held_as)


def setup_inputs(seed: int = 0) -> dict:
    key_list = jax.random.split(jax.random.key(seed), 6)
    return {
        "forward": heavy_noise(key_list[0], (SHOTS, SNAPS, COMPS, LEV, NX, NY), 1.0, 6.0, ((0, 2), (4, 4), (5, 4)), (0, 3, 2, 2.0)),
        "adjoint": scatter_about(key_list[1], (SHOTS, SNAPS, COMPS, LEV, NX, NY), 1.0, 6.0, ((0, 2), (4, 4), (5, 4))),
        "snap_times": draw_snap_times(jax.random.fold_in(key_list[5], 71), 0),
        "sources": plant(jax.random.randint(key_list[3], (SHOTS, 2), 0, min(NX, NY)), jax.random.fold_in(key_list[3], 1), 0, (min(NX, NY)) - 1).astype(jnp.int32),
        "aperture": plant((jax.random.randint(key_list[4], (SHOTS, N_GX, N_GY), 0, 4) < 3).astype(jnp.int32), jax.random.fold_in(key_list[4], 1), 0, 1),
    }


spread_x = 0.5
spread_y = 0.375


def kernel_weights(sigma):
    tap_list = jnp.arange(-RADIUS, RADIUS + 1).astype(jnp.float32)
    raw_taps = jnp.exp(-tap_list * tap_list / (2.0 * sigma * sigma))
    return raw_taps / jnp.sum(raw_taps)


def shot_gradient(forward_shot, adjoint_shot, steps_here, source, mask_tile):
    earlier = jnp.concatenate([jnp.zeros((1,), jnp.int32), steps_here[:-1]])
    weights = (steps_here - earlier).astype(jnp.float32) / 8.0
    gradient = jnp.zeros((3, LEV, NX, NY), jnp.float32)
    for which in range(SNAPS):
        forward_now = forward_shot[which]
        adjoint_now = adjoint_shot[which]

        def product(comp):
            return forward_now[comp].astype(jnp.float32) * adjoint_now[comp].astype(jnp.float32)

        density_term = product(0) + product(1) + product(2)
        trace_fwd = forward_now[3].astype(jnp.float32) + forward_now[4].astype(jnp.float32) + forward_now[5].astype(jnp.float32)
        trace_adj = adjoint_now[3].astype(jnp.float32) + adjoint_now[4].astype(jnp.float32) + adjoint_now[5].astype(jnp.float32)
        lame_term = trace_fwd * trace_adj
        shear_term = 2.0 * (product(3) + product(4) + product(5) + 2.0 * (product(6) + product(7) + product(8)))
        gradient = gradient + jnp.stack([lame_term, shear_term, density_term]) * (-weights[which])
    x_cells = jnp.arange(NX).astype(jnp.int32)
    y_cells = jnp.arange(NY).astype(jnp.int32)
    delta_x = (x_cells - source[0]).astype(jnp.float32)
    delta_y = (y_cells - source[1]).astype(jnp.float32)
    distance = (delta_x * delta_x)[:, None] + (delta_y * delta_y)[None, :]
    mask_cells = jnp.repeat(jnp.repeat(mask_tile, CX, 0), CY, 1).astype(jnp.float32)
    taper = (1.0 - jnp.exp(-distance / (2.0 * MUTE * MUTE))) * mask_cells
    return gradient * taper


def reference(forward, adjoint, snap_times, sources, aperture):
    def add_shot(carry, items):
        return carry + shot_gradient(*items), None

    start = jnp.zeros((3, LEV, NX, NY), jnp.float32)
    total, _ = lax.scan(add_shot, start, (forward, adjoint, snap_times, sources, aperture))
    weights_x = kernel_weights(spread_x * RADIUS)
    padded = jnp.pad(total, ((0, 0), (0, 0), (RADIUS, RADIUS), (0, 0)))
    along_x = jnp.zeros_like(total)
    for shift in range(2 * RADIUS + 1):
        along_x = along_x + weights_x[shift] * padded[:, :, shift:shift + NX, :]
    weights_y = kernel_weights(spread_y * RADIUS)
    padded = jnp.pad(along_x, ((0, 0), (0, 0), (0, 0), (RADIUS, RADIUS)))
    smoothed = jnp.zeros_like(total)
    for shift in range(2 * RADIUS + 1):
        smoothed = smoothed + weights_y[shift] * padded[:, :, :, shift:shift + NY]
    return smoothed
```

```python
import functools

import jax
import jax.numpy as jnp
import numpy as np
from jax import lax
from jax.experimental import pallas as pl
from jax.experimental.pallas import tpu as pltpu
from jax.sharding import PartitionSpec as P

RADIUS = 16
MUTE = 32
SIGMA_X = 0.5 * RADIUS
SIGMA_Y = 0.375 * RADIUS
ROWS = 16


def band_parts(count, sigma):
    taps = np.arange(-RADIUS, RADIUS + 1).astype(np.float64)
    norm = np.exp(-taps * taps / (2.0 * sigma * sigma)).sum()
    own = np.arange(count)
    cells = np.concatenate([own, np.arange(-RADIUS, 0), np.arange(count, count + RADIUS)])
    offset = (cells[:, None] - own[None, :]).astype(np.float64)
    values = np.exp(-offset * offset / (2.0 * sigma * sigma)) / norm
    values = np.where(np.abs(offset) <= RADIUS, values, 0.0).astype(np.float32)
    high = values.astype(jnp.bfloat16)
    low = (values - high.astype(np.float32)).astype(jnp.bfloat16)
    return np.concatenate([high, low], axis=1)


def kernel(
    n, ng, nh, raw,
    fwd, adj, times, sources, aperture, band_x, band_y,
    out,
    fbuf, abuf, taper, wx, wy, sm, recv,
    load_f, load_a, x_send, x_recv, gx_send, gx_recv, gy_send, gy_recv,
):
    me = lax.axis_index("shot")
    g = lax.axis_index("gx")
    h = lax.axis_index("gy")
    snaps = fwd.shape[1]
    levels = fwd.shape[3]
    width_x, width_y = fwd.shape[4], fwd.shape[5]
    here = levels // n
    peers = (n - 1) * here

    def load(q):
        level = lax.rem(me + q // here + 1, n) * here + lax.rem(q, here)
        return (
            pltpu.make_async_copy(fwd.at[0, :, :, level], fbuf.at[q], load_f.at[q]),
            pltpu.make_async_copy(adj.at[0, :, :, level], abuf.at[q], load_a.at[q]),
        )

    def start_load(q, c):
        for copy in load(q):
            copy.start()
        return c

    lax.fori_loop(0, levels, start_load, 0)

    barrier = pltpu.get_barrier_semaphore()
    for d in range(1, n):
        pl.semaphore_signal(barrier, inc=1, device_id={"shot": lax.rem(me + d, n)})
    greeted = jnp.int32(n - 1)
    for axis, at, count in (("gx", g, ng), ("gy", h, nh)):
        @pl.when(at > 0)
        def _():
            pl.semaphore_signal(barrier, inc=1, device_id={axis: at - 1})

        @pl.when(at < count - 1)
        def _():
            pl.semaphore_signal(barrier, inc=1, device_id={axis: at + 1})

        greeted = greeted + (at > 0).astype(jnp.int32) + (at < count - 1).astype(jnp.int32)

    for buf, at, count, width in ((wx, g, ng, width_x), (wy, h, nh, width_y)):
        for there, start in ((at > 0, width), (at < count - 1, width + RADIUS)):
            @pl.when(jnp.logical_not(there))
            def _():
                def clear(q, c):
                    buf[q, :, start:start + RADIUS, :] = jnp.zeros(
                        (3, RADIUS, buf.shape[3]), jnp.float32
                    )
                    return c

                lax.fori_loop(0, levels, clear, 0)

    x_at = g * width_x + lax.broadcasted_iota(jnp.int32, (width_x, width_y), 0)
    y_at = h * width_y + lax.broadcasted_iota(jnp.int32, (width_x, width_y), 1)
    dx = (x_at - sources[0, 0]).astype(jnp.float32)
    dy = (y_at - sources[0, 1]).astype(jnp.float32)
    taper[...] = (1.0 - jnp.exp(-(dx * dx + dy * dy) / (2.0 * MUTE * MUTE))) * aperture[
        0, 0, 0
    ].astype(jnp.float32)

    weights = []
    for k in range(snaps):
        step = times[0, k] - (times[0, k - 1] if k else 0)
        weights.append(step.astype(jnp.float32) * -0.125)

    def image(q):
        def rows_of(c, carry):
            rows = pl.ds(pl.multiple_of(c * ROWS, ROWS), ROWS)
            lame = shear = density = None
            for k in range(snaps):
                f = [fbuf[q, k, i, rows, :].astype(jnp.float32) for i in range(9)]
                a = [abuf[q, k, i, rows, :].astype(jnp.float32) for i in range(9)]
                w = weights[k]
                la = (f[3] + f[4] + f[5]) * (a[3] + a[4] + a[5]) * w
                sh = (
                    f[3] * a[3] + f[4] * a[4] + f[5] * a[5]
                    + 2.0 * (f[6] * a[6] + f[7] * a[7] + f[8] * a[8])
                ) * (2.0 * w)
                de = (f[0] * a[0] + f[1] * a[1] + f[2] * a[2]) * w
                if k == 0:
                    lame, shear, density = la, sh, de
                else:
                    lame, shear, density = lame + la, shear + sh, density + de
            t = taper[rows, :]
            wx[q, 0, rows, :] = lame * t
            wx[q, 1, rows, :] = shear * t
            wx[q, 2, rows, :] = density * t
            return carry

        lax.fori_loop(0, width_x // ROWS, rows_of, 0)

    def x_copy(src, q):
        d = q // here + 1
        return pltpu.make_async_remote_copy(
            src_ref=src,
            dst_ref=recv.at[q],
            send_sem=x_send.at[q],
            recv_sem=x_recv.at[q],
            device_id={"shot": lax.rem(me + d, n)},
        )

    def halo(axis, q):
        buf, at, count, width, send, recv_sem = (
            (wx, g, ng, width_x, gx_send, gx_recv)
            if axis == "gx"
            else (wy, h, nh, width_y, gy_send, gy_recv)
        )

        def copy(side):
            first = 0 if side == 0 else width - RADIUS
            lands = width + RADIUS if side == 0 else width
            other = lax.rem(at + (count - 1 if side == 0 else 1), count)
            return pltpu.make_async_remote_copy(
                src_ref=buf.at[q, :, pl.ds(first, RADIUS), :],
                dst_ref=buf.at[q, :, pl.ds(lands, RADIUS), :],
                send_sem=send.at[side, q],
                recv_sem=recv_sem.at[side, q],
                device_id={axis: other},
            )

        return copy, at > 0, at < count - 1

    def halo_start(axis, q):
        copy, left, right = halo(axis, q)
        pl.when(left)(lambda: copy(0).start())
        pl.when(right)(lambda: copy(1).start())

    def halo_arrived(axis, q):
        copy, left, right = halo(axis, q)
        pl.when(right)(lambda: copy(0).wait_recv())
        pl.when(left)(lambda: copy(1).wait_recv())

    def halo_sent(axis, q):
        copy, left, right = halo(axis, q)
        pl.when(left)(lambda: copy(0).wait_send())
        pl.when(right)(lambda: copy(1).wait_send())

    def smooth(cells, band):
        width = band.shape[1] // 2
        high = cells.astype(jnp.bfloat16)
        low = (cells - high.astype(jnp.float32)).astype(jnp.bfloat16)
        dims = (((0,), (0,)), ((), ()))
        both = lax.dot_general(high, band[...], dims, preferred_element_type=jnp.float32)
        rest = lax.dot_general(
            low, band[:, :width], dims, preferred_element_type=jnp.float32
        )
        return both[:, :width] + (both[:, width:] + rest)

    def along_x(q):
        halo_arrived("gx", q)
        for p in range(3):
            wy[q, p, 0:width_y, :] = smooth(wx[q, p], band_x)
        halo_start("gy", q)

    def is_raw(q):
        return lax.rem(q, here) < raw

    def make(q, c):
        for copy in load(q):
            copy.wait()
        image(q)

        @pl.when(q == 0)
        def _():
            pl.semaphore_wait(barrier, greeted)

        @pl.when(jnp.logical_and(is_raw(q), q < peers))
        def _():
            x_copy(wx.at[q, :, pl.ds(0, width_x), :], q).start()

        @pl.when(jnp.logical_not(is_raw(q)))
        def _():
            halo_start("gx", q)

        return c

    lax.fori_loop(0, levels, make, 0)

    def first_x(q, c):
        @pl.when(jnp.logical_not(is_raw(q)))
        def _():
            along_x(q)

        return c

    lax.fori_loop(0, levels, first_x, 0)

    def to_send(q, c):
        @pl.when(jnp.logical_not(is_raw(q)))
        def _():
            halo_arrived("gy", q)
            for p in range(3):
                sm[q, p] = smooth(wy[q, p], band_y)
            x_copy(sm.at[q], q).start()

        return c

    lax.fori_loop(0, peers, to_send, 0)

    def to_out(i, c):
        q = peers + i
        halo_arrived("gy", q)
        for p in range(3):
            out[p, i] = smooth(wy[q, p], band_y)
        return c

    lax.fori_loop(raw, here, to_out, 0)

    def sum_raw(i, c):
        for d in range(n - 1):
            q = d * here + i
            x_copy(wx.at[q, :, pl.ds(0, width_x), :], q).wait_recv()
        for p in range(3):
            total = wx[peers + i, p, 0:width_x, :]
            for d in range(n - 1):
                total = total + recv[d * here + i, p]
            wx[peers + i, p, 0:width_x, :] = total
        halo_start("gx", peers + i)
        return c

    lax.fori_loop(0, raw, sum_raw, 0)

    def raw_x(i, c):
        along_x(peers + i)
        return c

    lax.fori_loop(0, raw, raw_x, 0)
    lax.fori_loop(0, raw, to_out, 0)

    def add(i, c):
        for d in range(n - 1):
            q = d * here + i
            x_copy(sm.at[q], q).wait_recv()
        for p in range(3):
            total = out[p, i]
            for d in range(n - 1):
                total = total + recv[d * here + i, p]
            out[p, i] = total
        return c

    lax.fori_loop(raw, here, add, 0)

    def done(q, c):
        @pl.when(q < peers)
        def _():
            x_copy(sm.at[q], q).wait_send()

        @pl.when(jnp.logical_or(q >= peers, jnp.logical_not(is_raw(q))))
        def _():
            halo_sent("gx", q)
            halo_sent("gy", q)

        return c

    lax.fori_loop(0, levels, done, 0)


def on_device(n, ng, nh, forward, adjoint, snap_times, sources, aperture):
    snaps, comps, levels, width_x, width_y = forward.shape[1:]
    here = levels // n
    peers = (n - 1) * here
    raw = here // 2
    f32 = jnp.float32
    dma = pltpu.SemaphoreType.DMA
    smem = pl.BlockSpec(memory_space=pltpu.SMEM)
    vmem = pl.BlockSpec(memory_space=pltpu.VMEM)
    anywhere = pl.BlockSpec(memory_space=pl.ANY)
    return pl.pallas_call(
        functools.partial(kernel, n, ng, nh, raw),
        out_shape=jax.ShapeDtypeStruct((3, here, width_x, width_y), f32),
        in_specs=[anywhere, anywhere, smem, smem, smem, vmem, vmem],
        out_specs=vmem,
        scratch_shapes=[
            pltpu.VMEM((levels, snaps, comps, width_x, width_y), forward.dtype),
            pltpu.VMEM((levels, snaps, comps, width_x, width_y), adjoint.dtype),
            pltpu.VMEM((width_x, width_y), f32),
            pltpu.VMEM((levels, 3, width_x + 2 * RADIUS, width_y), f32),
            pltpu.VMEM((levels, 3, width_y + 2 * RADIUS, width_x), f32),
            pltpu.VMEM((peers, 3, width_x, width_y), f32),
            pltpu.VMEM((peers, 3, width_x, width_y), f32),
            dma((levels,)),
            dma((levels,)),
            dma((peers,)),
            dma((peers,)),
            dma((2, levels)),
            dma((2, levels)),
            dma((2, levels)),
            dma((2, levels)),
        ],
        compiler_params=pltpu.CompilerParams(
            collective_id=0, has_side_effects=True, vmem_limit_bytes=52 * 1024 * 1024
        ),
        cost_estimate=pl.CostEstimate(
            flops=2 * forward.size * 4,
            bytes_accessed=4 * forward.size + 12 * here * width_x * width_y,
            transcendentals=width_x * width_y,
        ),
    )(
        forward, adjoint, snap_times, sources, aperture,
        band_parts(width_x, SIGMA_X), band_parts(width_y, SIGMA_Y),
    )


def solution(mesh):
    in_specs = (
        P("shot", None, None, None, "gx", "gy"),
        P("shot", None, None, None, "gx", "gy"),
        P("shot", None),
        P("shot", None),
        P("shot", "gx", "gy"),
    )
    sizes = (mesh.shape["shot"], mesh.shape["gx"], mesh.shape["gy"])
    return jax.shard_map(
        functools.partial(on_device, *sizes),
        mesh=mesh,
        in_specs=in_specs,
        out_specs=P(None, "shot", "gx", "gy"),
        check_vma=False,
    )
```

```python
import functools

import jax
import jax.numpy as jnp
import numpy as np
from jax import lax
from jax.experimental import pallas as pl
from jax.experimental.pallas import tpu as pltpu
from jax.sharding import PartitionSpec as P

RADIUS = 16
MUTE = 32
SIGMA_X = 0.5 * RADIUS
SIGMA_Y = 0.375 * RADIUS
ROWS = 16
AHEAD = 3


def fill_band(band, sigma):
    count = band.shape[1] // 2
    taps = np.arange(-RADIUS, RADIUS + 1).astype(np.float64)
    norm = float(np.exp(-taps * taps / (2.0 * sigma * sigma)).sum())
    row = lax.broadcasted_iota(jnp.int32, (count + 2 * RADIUS, count), 0)
    own = lax.broadcasted_iota(jnp.int32, (count + 2 * RADIUS, count), 1)
    left = jnp.logical_and(row >= count, row < count + RADIUS)
    cell = jnp.where(row < count, row, jnp.where(left, row - count - RADIUS, row - RADIUS))
    offset = cell - own
    real = offset.astype(jnp.float32)
    values = jnp.exp(-real * real / (2.0 * sigma * sigma)) / norm
    values = jnp.where(jnp.abs(offset) <= RADIUS, values, 0.0)
    high = values.astype(jnp.bfloat16)
    band[:, :count] = high
    band[:, count:] = (values - high.astype(jnp.float32)).astype(jnp.bfloat16)


def kernel(
    n, ng, nh, raw,
    fwd, adj, scalars_in,
    out,
    scalars, band_x, band_y, fbuf, abuf, taper, wx, wy, sm, recv,
    small, load_f, load_a, x_send, x_recv, gx_send, gx_recv, gy_send, gy_recv,
):
    me = lax.axis_index("shot")
    g = lax.axis_index("gx")
    h = lax.axis_index("gy")
    snaps = fwd.shape[1]
    levels = fwd.shape[3]
    width_x, width_y = fwd.shape[4], fwd.shape[5]
    here = levels // n
    peers = (n - 1) * here

    def load(q):
        level = lax.rem(me + q // here + 1, n) * here + lax.rem(q, here)
        return (
            pltpu.make_async_copy(fwd.at[0, :, :, level], fbuf.at[q], load_f.at[q]),
            pltpu.make_async_copy(adj.at[0, :, :, level], abuf.at[q], load_a.at[q]),
        )

    def start_load(q, c):
        for copy in load(q):
            copy.start()
        return c

    ahead = min(AHEAD, levels)
    lax.fori_loop(0, 1, start_load, 0)
    fetch = pltpu.make_async_copy(scalars_in, scalars, small)
    fetch.start()
    lax.fori_loop(1, ahead, start_load, 0)

    barrier = pltpu.get_barrier_semaphore()
    for d in range(1, n):
        pl.semaphore_signal(barrier, inc=1, device_id={"shot": lax.rem(me + d, n)})
    greeted = jnp.int32(n - 1)
    for axis, at, count in (("gx", g, ng), ("gy", h, nh)):
        @pl.when(at > 0)
        def _():
            pl.semaphore_signal(barrier, inc=1, device_id={axis: at - 1})

        @pl.when(at < count - 1)
        def _():
            pl.semaphore_signal(barrier, inc=1, device_id={axis: at + 1})

        greeted = greeted + (at > 0).astype(jnp.int32) + (at < count - 1).astype(jnp.int32)

    for buf, at, count, width in ((wx, g, ng, width_x), (wy, h, nh, width_y)):
        for there, start in ((at > 0, width), (at < count - 1, width + RADIUS)):
            @pl.when(jnp.logical_not(there))
            def _():
                def clear(q, c):
                    buf[q, :, start:start + RADIUS, :] = jnp.zeros(
                        (3, RADIUS, buf.shape[3]), jnp.float32
                    )
                    return c

                lax.fori_loop(0, levels, clear, 0)

    fetch.wait()
    x_at = g * width_x + lax.broadcasted_iota(jnp.int32, (width_x, width_y), 0)
    y_at = h * width_y + lax.broadcasted_iota(jnp.int32, (width_x, width_y), 1)
    dx = (x_at - scalars[0, snaps]).astype(jnp.float32)
    dy = (y_at - scalars[0, snaps + 1]).astype(jnp.float32)
    taper[...] = (1.0 - jnp.exp(-(dx * dx + dy * dy) / (2.0 * MUTE * MUTE))) * scalars[
        0, snaps + 2
    ].astype(jnp.float32)

    fill_band(band_x, SIGMA_X)
    fill_band(band_y, SIGMA_Y)

    weights = []
    for k in range(snaps):
        step = scalars[0, k] - (scalars[0, k - 1] if k else 0)
        weights.append(step.astype(jnp.float32) * -0.125)

    def image(q):
        def rows_of(c, carry):
            rows = pl.ds(pl.multiple_of(c * ROWS, ROWS), ROWS)
            lame = shear = density = None
            for k in range(snaps):
                f = [fbuf[q, k, i, rows, :].astype(jnp.float32) for i in range(9)]
                a = [abuf[q, k, i, rows, :].astype(jnp.float32) for i in range(9)]
                w = weights[k]
                la = (f[3] + f[4] + f[5]) * (a[3] + a[4] + a[5]) * w
                sh = (
                    f[3] * a[3] + f[4] * a[4] + f[5] * a[5]
                    + 2.0 * (f[6] * a[6] + f[7] * a[7] + f[8] * a[8])
                ) * (2.0 * w)
                de = (f[0] * a[0] + f[1] * a[1] + f[2] * a[2]) * w
                if k == 0:
                    lame, shear, density = la, sh, de
                else:
                    lame, shear, density = lame + la, shear + sh, density + de
            t = taper[rows, :]
            wx[q, 0, rows, :] = lame * t
            wx[q, 1, rows, :] = shear * t
            wx[q, 2, rows, :] = density * t
            return carry

        lax.fori_loop(0, width_x // ROWS, rows_of, 0)

    def x_copy(src, q):
        d = q // here + 1
        return pltpu.make_async_remote_copy(
            src_ref=src,
            dst_ref=recv.at[q],
            send_sem=x_send.at[q],
            recv_sem=x_recv.at[q],
            device_id={"shot": lax.rem(me + d, n)},
        )

    def halo(axis, q):
        buf, at, count, width, send, recv_sem = (
            (wx, g, ng, width_x, gx_send, gx_recv)
            if axis == "gx"
            else (wy, h, nh, width_y, gy_send, gy_recv)
        )

        def copy(side):
            first = 0 if side == 0 else width - RADIUS
            lands = width + RADIUS if side == 0 else width
            other = lax.rem(at + (count - 1 if side == 0 else 1), count)
            return pltpu.make_async_remote_copy(
                src_ref=buf.at[q, :, pl.ds(first, RADIUS), :],
                dst_ref=buf.at[q, :, pl.ds(lands, RADIUS), :],
                send_sem=send.at[side, q],
                recv_sem=recv_sem.at[side, q],
                device_id={axis: other},
            )

        return copy, at > 0, at < count - 1

    def halo_start(axis, q):
        copy, left, right = halo(axis, q)
        pl.when(left)(lambda: copy(0).start())
        pl.when(right)(lambda: copy(1).start())

    def halo_arrived(axis, q):
        copy, left, right = halo(axis, q)
        pl.when(right)(lambda: copy(0).wait_recv())
        pl.when(left)(lambda: copy(1).wait_recv())

    def halo_sent(axis, q):
        copy, left, right = halo(axis, q)
        pl.when(left)(lambda: copy(0).wait_send())
        pl.when(right)(lambda: copy(1).wait_send())

    def smooth(cells, band):
        width = band.shape[1] // 2
        high = cells.astype(jnp.bfloat16)
        low = (cells - high.astype(jnp.float32)).astype(jnp.bfloat16)
        dims = (((0,), (0,)), ((), ()))
        both = lax.dot_general(high, band[...], dims, preferred_element_type=jnp.float32)
        rest = lax.dot_general(
            low, band[:, :width], dims, preferred_element_type=jnp.float32
        )
        return both[:, :width] + (both[:, width:] + rest)

    def along_x(q):
        halo_arrived("gx", q)
        for p in range(3):
            wy[q, p, 0:width_y, :] = smooth(wx[q, p], band_x)
        halo_start("gy", q)

    def is_raw(q):
        return lax.rem(q, here) < raw

    def make(q, c):
        @pl.when(q + ahead < levels)
        def _():
            start_load(q + ahead, 0)

        for copy in load(q):
            copy.wait()
        image(q)

        @pl.when(q == 0)
        def _():
            pl.semaphore_wait(barrier, greeted)

        @pl.when(jnp.logical_and(is_raw(q), q < peers))
        def _():
            x_copy(wx.at[q, :, pl.ds(0, width_x), :], q).start()

        @pl.when(jnp.logical_not(is_raw(q)))
        def _():
            halo_start("gx", q)

        return c

    lax.fori_loop(0, levels, make, 0)

    def first_x(q, c):
        @pl.when(jnp.logical_not(is_raw(q)))
        def _():
            along_x(q)

        return c

    lax.fori_loop(0, levels, first_x, 0)

    def to_send(q, c):
        @pl.when(jnp.logical_not(is_raw(q)))
        def _():
            halo_arrived("gy", q)
            for p in range(3):
                sm[q, p] = smooth(wy[q, p], band_y)
            x_copy(sm.at[q], q).start()

        return c

    lax.fori_loop(0, peers, to_send, 0)

    def to_out(i, c):
        q = peers + i
        halo_arrived("gy", q)
        for p in range(3):
            out[p, i] = smooth(wy[q, p], band_y)
        return c

    lax.fori_loop(raw, here, to_out, 0)

    def sum_raw(i, c):
        for d in range(n - 1):
            q = d * here + i
            x_copy(wx.at[q, :, pl.ds(0, width_x), :], q).wait_recv()
        for p in range(3):
            total = wx[peers + i, p, 0:width_x, :]
            for d in range(n - 1):
                total = total + recv[d * here + i, p]
            wx[peers + i, p, 0:width_x, :] = total
        halo_start("gx", peers + i)
        return c

    lax.fori_loop(0, raw, sum_raw, 0)

    def raw_x(i, c):
        along_x(peers + i)
        return c

    lax.fori_loop(0, raw, raw_x, 0)
    lax.fori_loop(0, raw, to_out, 0)

    def add(i, c):
        for d in range(n - 1):
            q = d * here + i
            x_copy(sm.at[q], q).wait_recv()
        for p in range(3):
            total = out[p, i]
            for d in range(n - 1):
                total = total + recv[d * here + i, p]
            out[p, i] = total
        return c

    lax.fori_loop(raw, here, add, 0)

    def done(q, c):
        @pl.when(q < peers)
        def _():
            x_copy(sm.at[q], q).wait_send()

        @pl.when(jnp.logical_or(q >= peers, jnp.logical_not(is_raw(q))))
        def _():
            halo_sent("gx", q)
            halo_sent("gy", q)

        return c

    lax.fori_loop(0, levels, done, 0)


def store(cells, out, sems):
    copies = [
        pltpu.make_async_copy(cells.at[p], out.at[p], sems.at[p]) for p in range(cells.shape[0])
    ]
    for copy in copies:
        copy.start()
    for copy in copies:
        copy.wait()


def on_device(n, ng, nh, forward, adjoint, snap_times, sources, aperture):
    snaps, comps, levels, width_x, width_y = forward.shape[1:]
    here = levels // n
    peers = (n - 1) * here
    raw = here // 2
    scalars = jnp.concatenate([snap_times, sources, aperture[:, :, 0]], axis=1)
    f32 = jnp.float32
    dma = pltpu.SemaphoreType.DMA
    vmem = pl.BlockSpec(memory_space=pltpu.VMEM)
    hbm = pl.BlockSpec(memory_space=pltpu.HBM)
    summed = pl.pallas_call(
        functools.partial(kernel, n, ng, nh, raw),
        out_shape=jax.ShapeDtypeStruct((3, here, width_x, width_y), f32),
        in_specs=[hbm, hbm, pl.BlockSpec(memory_space=pl.ANY)],
        out_specs=vmem,
        scratch_shapes=[
            pltpu.SMEM(scalars.shape, scalars.dtype),
            pltpu.VMEM((width_x + 2 * RADIUS, 2 * width_x), jnp.bfloat16),
            pltpu.VMEM((width_y + 2 * RADIUS, 2 * width_y), jnp.bfloat16),
            pltpu.VMEM((levels, snaps, comps, width_x, width_y), forward.dtype),
            pltpu.VMEM((levels, snaps, comps, width_x, width_y), adjoint.dtype),
            pltpu.VMEM((width_x, width_y), f32),
            pltpu.VMEM((levels, 3, width_x + 2 * RADIUS, width_y), f32),
            pltpu.VMEM((levels, 3, width_y + 2 * RADIUS, width_x), f32),
            pltpu.VMEM((peers, 3, width_x, width_y), f32),
            pltpu.VMEM((peers, 3, width_x, width_y), f32),
            dma,
            dma((levels,)),
            dma((levels,)),
            dma((peers,)),
            dma((peers,)),
            dma((2, levels)),
            dma((2, levels)),
            dma((2, levels)),
            dma((2, levels)),
        ],
        compiler_params=pltpu.CompilerParams(
            collective_id=0, has_side_effects=True, vmem_limit_bytes=52 * 1024 * 1024
        ),
        cost_estimate=pl.CostEstimate(
            flops=2 * forward.size * 4,
            bytes_accessed=4 * forward.size + 12 * here * width_x * width_y,
            transcendentals=width_x * width_y,
        ),
    )(
        forward, adjoint, scalars
    )
    return pl.pallas_call(
        store,
        out_shape=jax.ShapeDtypeStruct(summed.shape, summed.dtype),
        in_specs=[vmem],
        out_specs=hbm,
        scratch_shapes=[dma((3,))],
        compiler_params=pltpu.CompilerParams(vmem_limit_bytes=4 * 1024 * 1024),
    )(summed)


def solution(mesh):
    in_specs = (
        P("shot", None, None, None, "gx", "gy"),
        P("shot", None, None, None, "gx", "gy"),
        P("shot", None),
        P("shot", None),
        P("shot", "gx", "gy"),
    )
    sizes = (mesh.shape["shot"], mesh.shape["gx"], mesh.shape["gy"])
    return jax.shard_map(
        functools.partial(on_device, *sizes),
        mesh=mesh,
        in_specs=in_specs,
        out_specs=P(None, "shot", "gx", "gy"),
        check_vma=False,
    )
```

```python
import functools

import jax
import jax.numpy as jnp
import numpy as np
from jax import lax
from jax.experimental import pallas as pl
from jax.experimental.pallas import tpu as pltpu
from jax.sharding import PartitionSpec as P

RADIUS = 16
MUTE = 32
SIGMA_X = 0.5 * RADIUS
SIGMA_Y = 0.375 * RADIUS
ROWS = 16
AHEAD = 3


def fill_band(band, sigma):
    count = band.shape[1] // 2
    taps = np.arange(-RADIUS, RADIUS + 1).astype(np.float64)
    norm = float(np.exp(-taps * taps / (2.0 * sigma * sigma)).sum())
    row = lax.broadcasted_iota(jnp.int32, (count + 2 * RADIUS, count), 0)
    own = lax.broadcasted_iota(jnp.int32, (count + 2 * RADIUS, count), 1)
    left = jnp.logical_and(row >= count, row < count + RADIUS)
    cell = jnp.where(row < count, row, jnp.where(left, row - count - RADIUS, row - RADIUS))
    offset = cell - own
    real = offset.astype(jnp.float32)
    values = jnp.exp(-real * real / (2.0 * sigma * sigma)) / norm
    values = jnp.where(jnp.abs(offset) <= RADIUS, values, 0.0)
    high = values.astype(jnp.bfloat16)
    band[:, :count] = high
    band[:, count:] = (values - high.astype(jnp.float32)).astype(jnp.bfloat16)


def kernel(
    n, ng, nh, raw,
    fwd, adj, scalars_in,
    out,
    scalars, band_x, band_y, fbuf, abuf, taper, wx, wy, sm, recv,
    small, load_f, load_a, x_send, x_recv, gx_send, gx_recv, gy_send, gy_recv,
):
    me = lax.axis_index("shot")
    g = lax.axis_index("gx")
    h = lax.axis_index("gy")
    snaps = fwd.shape[1]
    levels = fwd.shape[3]
    width_x, width_y = fwd.shape[4], fwd.shape[5]
    here = levels // n
    peers = (n - 1) * here

    barrier = pltpu.get_barrier_semaphore()
    for d in range(1, n):
        pl.semaphore_signal(barrier, inc=1, device_id={"shot": lax.rem(me + d, n)})
    greeted = jnp.int32(n - 1)
    for axis, at, count in (("gx", g, ng), ("gy", h, nh)):
        @pl.when(at > 0)
        def _():
            pl.semaphore_signal(barrier, inc=1, device_id={axis: at - 1})

        @pl.when(at < count - 1)
        def _():
            pl.semaphore_signal(barrier, inc=1, device_id={axis: at + 1})

        greeted = greeted + (at > 0).astype(jnp.int32) + (at < count - 1).astype(jnp.int32)

    def load(q):
        level = lax.rem(me + q // here + 1, n) * here + lax.rem(q, here)
        return (
            pltpu.make_async_copy(fwd.at[0, :, :, level], fbuf.at[q], load_f.at[q]),
            pltpu.make_async_copy(adj.at[0, :, :, level], abuf.at[q], load_a.at[q]),
        )

    def start_load(q, c):
        for copy in load(q):
            copy.start()
        return c

    ahead = min(AHEAD, levels)
    lax.fori_loop(0, 1, start_load, 0)
    fetch = pltpu.make_async_copy(scalars_in, scalars, small)
    fetch.start()
    lax.fori_loop(1, ahead, start_load, 0)

    fetch.wait()
    x_at = g * width_x + lax.broadcasted_iota(jnp.int32, (width_x, width_y), 0)
    y_at = h * width_y + lax.broadcasted_iota(jnp.int32, (width_x, width_y), 1)
    dx = (x_at - scalars[0, snaps]).astype(jnp.float32)
    dy = (y_at - scalars[0, snaps + 1]).astype(jnp.float32)
    taper[...] = (1.0 - jnp.exp(-(dx * dx + dy * dy) / (2.0 * MUTE * MUTE))) * scalars[
        0, snaps + 2
    ].astype(jnp.float32)

    weights = []
    for k in range(snaps):
        step = scalars[0, k] - (scalars[0, k - 1] if k else 0)
        weights.append(step.astype(jnp.float32) * -0.125)

    def image(q):
        def rows_of(c, carry):
            rows = pl.ds(pl.multiple_of(c * ROWS, ROWS), ROWS)
            lame = shear = density = None
            for k in range(snaps):
                f = [fbuf[q, k, i, rows, :].astype(jnp.float32) for i in range(9)]
                a = [abuf[q, k, i, rows, :].astype(jnp.float32) for i in range(9)]
                w = weights[k]
                la = (f[3] + f[4] + f[5]) * (a[3] + a[4] + a[5]) * w
                sh = (
                    f[3] * a[3] + f[4] * a[4] + f[5] * a[5]
                    + 2.0 * (f[6] * a[6] + f[7] * a[7] + f[8] * a[8])
                ) * (2.0 * w)
                de = (f[0] * a[0] + f[1] * a[1] + f[2] * a[2]) * w
                if k == 0:
                    lame, shear, density = la, sh, de
                else:
                    lame, shear, density = lame + la, shear + sh, density + de
            t = taper[rows, :]
            wx[q, 0, rows, :] = lame * t
            wx[q, 1, rows, :] = shear * t
            wx[q, 2, rows, :] = density * t
            return carry

        lax.fori_loop(0, width_x // ROWS, rows_of, 0)

    def x_copy(src, q):
        d = q // here + 1
        return pltpu.make_async_remote_copy(
            src_ref=src,
            dst_ref=recv.at[q],
            send_sem=x_send.at[q],
            recv_sem=x_recv.at[q],
            device_id={"shot": lax.rem(me + d, n)},
        )

    def halo(axis, q):
        buf, at, count, width, send, recv_sem = (
            (wx, g, ng, width_x, gx_send, gx_recv)
            if axis == "gx"
            else (wy, h, nh, width_y, gy_send, gy_recv)
        )

        def copy(side):
            first = 0 if side == 0 else width - RADIUS
            lands = width + RADIUS if side == 0 else width
            other = lax.rem(at + (count - 1 if side == 0 else 1), count)
            return pltpu.make_async_remote_copy(
                src_ref=buf.at[q, :, pl.ds(first, RADIUS), :],
                dst_ref=buf.at[q, :, pl.ds(lands, RADIUS), :],
                send_sem=send.at[side, q],
                recv_sem=recv_sem.at[side, q],
                device_id={axis: other},
            )

        return copy, at > 0, at < count - 1

    def halo_start(axis, q):
        copy, left, right = halo(axis, q)
        pl.when(left)(lambda: copy(0).start())
        pl.when(right)(lambda: copy(1).start())

    def halo_arrived(axis, q):
        copy, left, right = halo(axis, q)
        pl.when(right)(lambda: copy(0).wait_recv())
        pl.when(left)(lambda: copy(1).wait_recv())

    def halo_sent(axis, q):
        copy, left, right = halo(axis, q)
        pl.when(left)(lambda: copy(0).wait_send())
        pl.when(right)(lambda: copy(1).wait_send())

    def smooth(cells, band):
        width = band.shape[1] // 2
        high = cells.astype(jnp.bfloat16)
        low = (cells - high.astype(jnp.float32)).astype(jnp.bfloat16)
        dims = (((0,), (0,)), ((), ()))
        both = lax.dot_general(high, band[...], dims, preferred_element_type=jnp.float32)
        rest = lax.dot_general(
            low, band[:, :width], dims, preferred_element_type=jnp.float32
        )
        return both[:, :width] + (both[:, width:] + rest)

    def along_x(q):
        halo_arrived("gx", q)
        for p in range(3):
            wy[q, p, 0:width_y, :] = smooth(wx[q, p], band_x)
        halo_start("gy", q)

    def is_raw(q):
        return lax.rem(q, here) < raw

    def make(q, c):
        @pl.when(q + ahead < levels)
        def _():
            start_load(q + ahead, 0)

        for copy in load(q):
            copy.wait()
        image(q)

        @pl.when(q == 0)
        def _():
            pl.semaphore_wait(barrier, greeted)

        @pl.when(jnp.logical_and(is_raw(q), q < peers))
        def _():
            x_copy(wx.at[q, :, pl.ds(0, width_x), :], q).start()

        @pl.when(jnp.logical_not(is_raw(q)))
        def _():
            halo_start("gx", q)

        return c

    lax.fori_loop(0, levels, make, 0)

    for buf, at, count, width in ((wx, g, ng, width_x), (wy, h, nh, width_y)):
        for there, start in ((at > 0, width), (at < count - 1, width + RADIUS)):
            @pl.when(jnp.logical_not(there))
            def _():
                def clear(q, c):
                    buf[q, :, start:start + RADIUS, :] = jnp.zeros(
                        (3, RADIUS, buf.shape[3]), jnp.float32
                    )
                    return c

                lax.fori_loop(0, levels, clear, 0)

    fill_band(band_x, SIGMA_X)
    fill_band(band_y, SIGMA_Y)

    def first_x(q, c):
        @pl.when(jnp.logical_not(is_raw(q)))
        def _():
            along_x(q)

        return c

    lax.fori_loop(0, levels, first_x, 0)

    def to_send(q, c):
        @pl.when(jnp.logical_not(is_raw(q)))
        def _():
            halo_arrived("gy", q)
            for p in range(3):
                sm[q, p] = smooth(wy[q, p], band_y)
            x_copy(sm.at[q], q).start()

        return c

    lax.fori_loop(0, peers, to_send, 0)

    def to_out(i, c):
        q = peers + i
        halo_arrived("gy", q)
        for p in range(3):
            out[p, i] = smooth(wy[q, p], band_y)
        return c

    lax.fori_loop(raw, here, to_out, 0)

    def sum_raw(i, c):
        for d in range(n - 1):
            q = d * here + i
            x_copy(wx.at[q, :, pl.ds(0, width_x), :], q).wait()
        for p in range(3):
            total = wx[peers + i, p, 0:width_x, :]
            for d in range(n - 1):
                total = total + recv[d * here + i, p]
            wx[peers + i, p, 0:width_x, :] = total
        halo_start("gx", peers + i)
        return c

    lax.fori_loop(0, raw, sum_raw, 0)

    def raw_x(i, c):
        along_x(peers + i)
        return c

    lax.fori_loop(0, raw, raw_x, 0)
    lax.fori_loop(0, raw, to_out, 0)

    def done(q, c):
        @pl.when(jnp.logical_or(q >= peers, jnp.logical_not(is_raw(q))))
        def _():
            halo_sent("gx", q)
            halo_sent("gy", q)

        return c

    lax.fori_loop(0, levels, done, 0)

    def add(i, c):
        for d in range(n - 1):
            q = d * here + i
            x_copy(sm.at[q], q).wait()
        for p in range(3):
            total = out[p, i]
            for d in range(n - 1):
                total = total + recv[d * here + i, p]
            out[p, i] = total
        return c

    lax.fori_loop(raw, here, add, 0)


def store(cells, out, sems):
    copies = [
        pltpu.make_async_copy(cells.at[p], out.at[p], sems.at[p]) for p in range(cells.shape[0])
    ]
    for copy in copies:
        copy.start()
    for copy in copies:
        copy.wait()


def on_device(n, ng, nh, forward, adjoint, snap_times, sources, aperture):
    snaps, comps, levels, width_x, width_y = forward.shape[1:]
    here = levels // n
    peers = (n - 1) * here
    raw = here // 2
    scalars = jnp.concatenate([snap_times, sources, aperture[:, :, 0]], axis=1)
    f32 = jnp.float32
    dma = pltpu.SemaphoreType.DMA
    vmem = pl.BlockSpec(memory_space=pltpu.VMEM)
    hbm = pl.BlockSpec(memory_space=pltpu.HBM)
    summed = pl.pallas_call(
        functools.partial(kernel, n, ng, nh, raw),
        out_shape=jax.ShapeDtypeStruct((3, here, width_x, width_y), f32),
        in_specs=[hbm, hbm, pl.BlockSpec(memory_space=pl.ANY)],
        out_specs=vmem,
        scratch_shapes=[
            pltpu.SMEM(scalars.shape, scalars.dtype),
            pltpu.VMEM((width_x + 2 * RADIUS, 2 * width_x), jnp.bfloat16),
            pltpu.VMEM((width_y + 2 * RADIUS, 2 * width_y), jnp.bfloat16),
            pltpu.VMEM((levels, snaps, comps, width_x, width_y), forward.dtype),
            pltpu.VMEM((levels, snaps, comps, width_x, width_y), adjoint.dtype),
            pltpu.VMEM((width_x, width_y), f32),
            pltpu.VMEM((levels, 3, width_x + 2 * RADIUS, width_y), f32),
            pltpu.VMEM((levels, 3, width_y + 2 * RADIUS, width_x), f32),
            pltpu.VMEM((peers, 3, width_x, width_y), f32),
            pltpu.VMEM((peers, 3, width_x, width_y), f32),
            dma,
            dma((levels,)),
            dma((levels,)),
            dma((peers,)),
            dma((peers,)),
            dma((2, levels)),
            dma((2, levels)),
            dma((2, levels)),
            dma((2, levels)),
        ],
        compiler_params=pltpu.CompilerParams(
            collective_id=0, has_side_effects=True, vmem_limit_bytes=52 * 1024 * 1024
        ),
        cost_estimate=pl.CostEstimate(
            flops=2 * forward.size * 4,
            bytes_accessed=4 * forward.size + 12 * here * width_x * width_y,
            transcendentals=width_x * width_y,
        ),
    )(
        forward, adjoint, scalars
    )
    return pl.pallas_call(
        store,
        out_shape=jax.ShapeDtypeStruct(summed.shape, summed.dtype),
        in_specs=[vmem],
        out_specs=hbm,
        scratch_shapes=[dma((3,))],
        compiler_params=pltpu.CompilerParams(vmem_limit_bytes=4 * 1024 * 1024),
    )(summed)


def solution(mesh):
    in_specs = (
        P("shot", None, None, None, "gx", "gy"),
        P("shot", None, None, None, "gx", "gy"),
        P("shot", None),
        P("shot", None),
        P("shot", "gx", "gy"),
    )
    sizes = (mesh.shape["shot"], mesh.shape["gx"], mesh.shape["gy"])
    return jax.shard_map(
        functools.partial(on_device, *sizes),
        mesh=mesh,
        in_specs=in_specs,
        out_specs=P(None, "shot", "gx", "gy"),
        check_vma=False,
    )
```
